256 devices in a mesh: gx: 8 (over x, core), gy: 32 (over y, z).
Axes of the slice: x: 4, y: 4, z: 8, core: 2. Of those that a mesh axis runs over, the one named last changes fastest.
Arguments:
- tokens: bfloat16 [512, 16384], P(None, ('gx', 'gy')), may hold values from -6 to 6
- gate_weight: bfloat16 [16384, 32768], P('gx', 'gy'), may hold values from -0.046875 to 0.046875
- up_weight: bfloat16 [16384, 32768], P('gx', 'gy'), may hold values from -0.046875 to 0.046875
- down_weight: bfloat16 [32, 1024, 16384], P(None, 'gx', 'gy'), may hold values from -0.03125 to 0.03125
Outputs:
- mixed: bfloat16 [512, 16384], P('gx', 'gy')
The draws below stay inside these ranges and needn't reach their ends.
All inputs are finite; a program needn't handle non-finite values.
Results may differ from the reference program's by a relative error of at most 0.005.
Values may be sent and summed in bfloat16 or wider, within the bound.
A program may use at most 64 MiB of HBM per device.

```python
import jax
import jax.numpy as jnp

D = 16384
FF = 32768
ROWS = 512
FOLD = 32


def level_of(own_key, shape, pieces, low, largest):
    gain = 1.0
    for dim, parts in pieces:
        steps = jax.random.uniform(jax.random.fold_in(jax.random.fold_in(own_key, 6), dim), (parts,), jnp.float32, low / len(pieces), largest / len(pieces))
        gain = gain * jnp.repeat(jnp.exp(steps), shape[dim] // parts).reshape((-1,) + (1,) * (len(shape) - 1 - dim))
    return gain


def bell_draw(own_key, dims, spread, reach, split=(), held_as=jnp.bfloat16):
    result = spread * jax.random.normal(own_key, dims, jnp.float32)
    if split:
        result = result * level_of(own_key, dims, split, -0.22, 0.18)
    return jnp.clip(result, -reach, reach).astype(held_as)


def setup_inputs(seed: int = 0) -> dict:
    seeds = jax.random.split(jax.random.key(seed), 5)
    return {
        "tokens": bell_draw(seeds[0], (ROWS, D), 1.0, 6.0, ((1, 256),)),
        "gate_weight": bell_draw(seeds[1], (D, FF), D ** -0.5, 0.046875, ((0, 8), (1, 32))),
        "up_weight": bell_draw(seeds[2], (D, FF), D ** -0.5, 0.046875, ((0, 8), (1, 32))),
        "down_weight": bell_draw(seeds[3], (FOLD, FF // FOLD, D), FF ** -0.5, 0.03125, ((1, 8), (2, 32))),
    }


def reference(tokens, gate_weight, up_weight, down_weight):
    gate = jnp.dot(tokens, gate_weight, preferred_element_type=jnp.float32)
    up = jnp.dot(tokens, up_weight, preferred_element_type=jnp.float32)
    hidden = (jax.nn.silu(gate) * up).astype(jnp.bfloat16)
    flat = down_weight.reshape(FF, D)
    return jnp.dot(hidden, flat, preferred_element_type=jnp.float32).astype(jnp.bfloat16)
```

```python
import functools

import jax
import jax.numpy as jnp
from jax import lax
from jax.experimental import pallas as pl
from jax.experimental.pallas import tpu as pltpu
from jax.sharding import PartitionSpec as P

MESH = pl.DeviceIdType.MESH
NX, NC, NY, NZ = 4, 2, 4, 8
CHUNKS = 4
ROWS = 128
HALF = ROWS // 2
PK = HALF // 2
SEMS = 320

RING4 = [[(0, 1, None), (0, -1, None)], [(-1, 1, 0), (1, -1, 1)]]
RING8 = [
    [(0, 1, None), (0, -1, None)],
    [(-1, 1, None), (1, -1, None)],
    [(-2, 1, None), (2, -1, None)],
    [(-3, 1, 0), (3, -1, 1)],
]
FAST4 = [[(0, 2, None), (0, 1, None), (0, -1, None)]]
FAST8 = [
    [(0, 2, None), (0, -2, None), (0, 1, None), (0, -1, None)],
    [(-2, 2, 0), (2, -2, 1), (-2, 1, None), (2, -1, None)],
]


def kernel(
    tok_hbm, gate_hbm, up_hbm, down_hbm, out_ref,
    tok, w1, wd, tok_p, tok_q, lhs, own, part_out, part_in, sum_out, sum_in,
    hid_p, hid_q, acc, acc_in, red_out, red_in,
    load_sem, send_sem, recv_sem,
):
    gx, gy = lax.axis_index("gx"), lax.axis_index("gy")
    x, core, y, z = gx // NC, gx % NC, gy // NZ, gy % NZ

    def at(dx=0, dc=0, dy=0, dz=0):
        return (
            (x + dx + NX) % NX * NC + (core + dc) % NC,
            (y + dy + NY) % NY * NZ + (z + dz + NZ) % NZ,
        )

    started = []

    def send(src, dst, device):
        k = len(started)
        copy = pltpu.make_async_remote_copy(
            src_ref=src, dst_ref=dst, send_sem=send_sem.at[k], recv_sem=recv_sem.at[k],
            device_id=device, device_id_type=MESH,
        )
        copy.start()
        started.append(copy)
        return copy

    load = pltpu.make_async_copy(tok_hbm, tok, load_sem.at[0])
    load.start()
    w_loads = []
    for slot in range(8):
        dc, dx = (1 - slot // 4), slot % 4
        share = (x + dx) % NX * NC + (core + dc) % NC
        columns = pl.ds(pl.multiple_of(share * 128, 128), 128)
        for h, src in enumerate((gate_hbm, up_hbm)):
            copy = pltpu.make_async_copy(
                src.at[:, columns], w1.at[slot, :, pl.ds(h * 128, 128)], load_sem.at[2 + 2 * slot + h]
            )
            copy.start()
            w_loads.append(copy)
    wd_load = pltpu.make_async_copy(down_hbm, wd, load_sem.at[1])
    wd_load.start()

    barrier = pltpu.get_barrier_semaphore()
    peers = [at(dy=d) for d in (1, -1, 2)] + [at(dz=d) for d in (1, -1, 2, -2)]
    peers += [at(dx=d) for d in (1, 2, 3)] + [at(dc=1)]
    for peer in peers:
        pl.semaphore_signal(barrier, inc=1, device_id=peer, device_id_type=MESH)

    load.wait()
    for ch in range(CHUNKS):
        side = []
        for c in range(NC):
            side.append(jnp.concatenate(
                [tok[(i * NC + c) * 64 + ch * 16:(i * NC + c) * 64 + ch * 16 + 16, :] for i in range(NX)], axis=0
            ))
        packed = jnp.concatenate(side, axis=1)
        tok_p[ch, z, y] = packed[:PK]
        tok_q[ch, y, z] = packed[PK:]
    pl.semaphore_wait(barrier, len(peers))

    def halved(ref, lead, half, size):
        if half is None:
            return ref.at[lead]
        return ref.at[lead + (pl.ds(half * size // 2, size // 2),)]

    class Gather:
        def __init__(self, ref, ch, first, plans, rows):
            self.ref, self.ch, self.first, self.rows = ref, ch, first, rows
            self.steps = [(0, s) for s in plans[0]] + [(1, s) for s in plans[1]]
            self.next = 0
            self.flying = []

        def start(self):
            phase, step = self.steps[self.next]
            self.next += 1
            along_y = (phase == 0) == (self.first == "y")
            n, me = (NY, y) if along_y else (NZ, z)
            for source, shift, half in step:
                block = (me + source + n) % n
                if phase == 0:
                    lead = (self.ch, z, block) if along_y else (self.ch, y, block)
                    part = halved(self.ref, lead, half, self.rows)
                else:
                    size = NZ if along_y else NY
                    part = halved(self.ref, (self.ch, block), half, size)
                device = at(dy=shift) if along_y else at(dz=shift)
                self.flying.append(send(part, part, device))

        def wait(self):
            for copy in self.flying:
                copy.wait_recv()
            self.flying = []

        def advance(self):
            self.wait()
            if self.next < len(self.steps):
                self.start()

    tok_plans = (FAST4, FAST8)
    gp = [Gather(tok_p, ch, "y", (tok_plans[0], tok_plans[1]), PK) for ch in range(CHUNKS)]
    gq = [Gather(tok_q, ch, "z", (tok_plans[1], tok_plans[0]), PK) for ch in range(CHUNKS)]
    hp = [Gather(hid_p, ch, "y", (RING4, RING8), HALF) for ch in range(CHUNKS)]
    hq = [Gather(hid_q, ch, "z", (RING8, RING4), HALF) for ch in range(CHUNKS)]

    summing = [[] for _ in range(CHUNKS)]

    def project(ch):
        gp[ch].wait()
        gq[ch].wait()
        for b in range(NY):
            for a in range(0, NZ, 2):
                for first, ref in ((0, tok_p.at[ch, a:a + 2, b]), (PK, tok_q.at[ch, b, a:a + 2])):
                    lo, hi = ref[0], ref[1]
                    columns = slice((b * NZ + a) * 64, (b * NZ + a) * 64 + 128)
                    lhs[first:first + PK, columns] = jnp.concatenate([lo[:, :64], hi[:, :64]], axis=1)
                    lhs[HALF + first:HALF + first + PK, columns] = jnp.concatenate([lo[:, 64:], hi[:, 64:]], axis=1)
        partner = [None] * 4
        for i in (2, 1, 3, 0):
            if ch == 0:
                w_loads[2 * i].wait()
                w_loads[2 * i + 1].wait()
            part_out[ch, i] = jnp.dot(lhs[...], w1[i], preferred_element_type=jnp.float32)
            partner[i] = send(part_out.at[ch, i], part_in.at[ch, i], at(dc=1))
        for i in (2, 1, 3, 0):
            if ch == 0:
                w_loads[8 + 2 * i].wait()
                w_loads[8 + 2 * i + 1].wait()
            mine = jnp.dot(lhs[...], w1[4 + i], preferred_element_type=jnp.float32)
            partner[i].wait_recv()
            mine = mine + part_in[ch, i]
            if i == 0:
                own[ch] = mine
            else:
                sum_out[ch, i - 1] = mine.astype(jnp.bfloat16)
                summing[ch].append(send(sum_out.at[ch, i - 1], sum_in.at[ch, i - 1], at(dx=i)))

    def activate(ch):
        for copy in summing[ch]:
            copy.wait_recv()
        total = own[ch]
        for i in range(3):
            total = total + sum_in[ch, i].astype(jnp.float32)
        gate, up = total[:, :128], total[:, 128:]
        hidden = (gate / (1.0 + jnp.exp(-gate)) * up).astype(jnp.bfloat16)
        hid_p[ch, z, y] = hidden[:HALF]
        hid_q[ch, y, z] = hidden[HALF:]
        hp[ch].start()
        hq[ch].start()

    mixing = [None] * CHUNKS
    reducing = [[] for _ in range(CHUNKS)]

    def mix(ch):
        if ch == 0:
            wd_load.wait()
        left = jnp.concatenate([hid_p[ch, a, b] for b in range(NY) for a in range(NZ)], axis=1)
        right = jnp.concatenate([hid_q[ch, b, a] for b in range(NY) for a in range(NZ)], axis=1)
        rows = jnp.concatenate([left, right], axis=0)
        acc[ch] = jnp.dot(rows, wd[...].reshape(NY * NZ * 128, 512), preferred_element_type=jnp.float32)
        theirs = pl.ds(pl.multiple_of((1 - core) * HALF, HALF), HALF)
        mixing[ch] = send(acc.at[ch, theirs], acc_in.at[ch], at(dc=1))

    def scatter(ch):
        mixing[ch].wait_recv()
        for i in (2, 1, 3, 0):
            place = (x + i) % NX * 16
            rows = pl.ds(pl.multiple_of(core * HALF + place, 16), 16)
            total = acc[ch, rows, :] + acc_in[ch, pl.ds(pl.multiple_of(place, 16), 16), :]
            if i == 0:
                acc[ch, rows, :] = total
            else:
                red_out[ch, i - 1] = total.astype(jnp.bfloat16)
                reducing[ch].append(send(red_out.at[ch, i - 1], red_in.at[ch, i - 1], at(dx=i)))

    def finish(ch):
        for copy in reducing[ch]:
            copy.wait_recv()
        rows = pl.ds(pl.multiple_of(core * HALF + x * 16, 16), 16)
        total = acc[ch, rows, :]
        for i in range(3):
            total = total + red_in[ch, i].astype(jnp.float32)
        out_ref[ch * 16:(ch + 1) * 16, :] = total.astype(jnp.bfloat16)

    for ch in range(CHUNKS):
        gp[ch].start()
        gq[ch].start()
    for step in range(1, max(len(gp[0].steps), len(gq[0].steps))):
        for ch in range(CHUNKS):
            gp[ch].advance()
            gq[ch].advance()
    for ch in range(CHUNKS):
        project(ch)
    for t in range(2 * CHUNKS + 7):
        for ch in range(CHUNKS):
            k = t - 2 * ch
            if k == 0:
                activate(ch)
            elif 1 <= k <= 6:
                hp[ch].advance()
                hq[ch].advance()
                if k == 6:
                    mix(ch)
            if k == 7:
                scatter(ch)
                if ch > 0:
                    finish(ch - 1)
    finish(CHUNKS - 1)

    for copy in started:
        copy.wait_send()


def body(tokens, gate_weight, up_weight, down_weight):
    bf16, f32 = jnp.bfloat16, jnp.float32
    return pl.pallas_call(
        kernel,
        out_shape=jax.ShapeDtypeStruct((64, 512), bf16),
        in_specs=[pl.BlockSpec(memory_space=pl.ANY)] * 4,
        out_specs=pl.BlockSpec(memory_space=pltpu.VMEM),
        scratch_shapes=[
            pltpu.VMEM((512, 64), bf16),
            pltpu.VMEM((8, 2048, 256), bf16),
            pltpu.VMEM((32, 128, 512), bf16),
            pltpu.VMEM((CHUNKS, NZ, NY, PK, 128), bf16),
            pltpu.VMEM((CHUNKS, NY, NZ, PK, 128), bf16),
            pltpu.VMEM((ROWS, 2048), bf16),
            pltpu.VMEM((CHUNKS, ROWS, 256), f32),
            pltpu.VMEM((CHUNKS, 4, ROWS, 256), f32),
            pltpu.VMEM((CHUNKS, 4, ROWS, 256), f32),
            pltpu.VMEM((CHUNKS, 3, ROWS, 256), bf16),
            pltpu.VMEM((CHUNKS, 3, ROWS, 256), bf16),
            pltpu.VMEM((CHUNKS, NZ, NY, HALF, 128), bf16),
            pltpu.VMEM((CHUNKS, NY, NZ, HALF, 128), bf16),
            pltpu.VMEM((CHUNKS, ROWS, 512), f32),
            pltpu.VMEM((CHUNKS, HALF, 512), f32),
            pltpu.VMEM((CHUNKS, 3, 16, 512), bf16),
            pltpu.VMEM((CHUNKS, 3, 16, 512), bf16),
            pltpu.SemaphoreType.DMA((18,)),
            pltpu.SemaphoreType.DMA((SEMS,)),
            pltpu.SemaphoreType.DMA((SEMS,)),
        ],
        compiler_params=pltpu.CompilerParams(
            collective_id=0, has_side_effects=True, vmem_limit_bytes=56 * 1024 * 1024
        ),
        cost_estimate=pl.CostEstimate(flops=6442450944, bytes_accessed=12 << 20, transcendentals=0),
    )(tokens, gate_weight, up_weight, down_weight)


def solution(mesh):
    in_specs = (P(None, ("gx", "gy")), P("gx", "gy"), P("gx", "gy"), P(None, "gx", "gy"))
    return jax.shard_map(body, mesh=mesh, in_specs=in_specs, out_specs=P("gx", "gy"), check_vma=False)
```

```python
import jax
import jax.numpy as jnp
from jax import lax
from jax.experimental import pallas as pl
from jax.experimental.pallas import tpu as pltpu
from jax.sharding import PartitionSpec as P

MESH = pl.DeviceIdType.MESH
NX, NC, NY, NZ = 4, 2, 4, 8
CHUNKS = 4
ROWS = 128
HALF = ROWS // 2
TOK_CUTS = (32, 32, 32, 32)
HID_CUTS = (48, 48, 48, 48)


def wrap(d, n):
    d %= n
    return d - n if d > n // 2 else d


def toward(d, n, jump, flip):
    if flip and d == n // 2:
        d = -d
    sign = 1 if d > 0 else -1
    size = abs(d)
    if jump == "all":
        return 0
    if jump == "two":
        return 0 if size <= 2 else sign * 2
    return sign * (size - 1)


def tree(first, jump_y, jump_z):
    parent, stage = {}, {(0, 0): 0}

    def visit(dy, dz):
        if (dy, dz) in stage:
            return stage[dy, dz]
        along_y = (dy != 0) if first == "z" else (dz == 0)
        if along_y:
            up = (wrap(toward(dy, NY, jump_y, dz % 2 == 1), NY), dz)
        else:
            up = (dy, wrap(toward(dz, NZ, jump_z, dy % 2 == 1), NZ))
        parent[dy, dz] = up
        stage[dy, dz] = visit(*up) + 1
        return stage[dy, dz]

    for dy in range(NY):
        for dz in range(NZ):
            visit(wrap(dy, NY), wrap(dz, NZ))
    count = max(stage.values())
    return parent, [sorted((b for b in stage if stage[b] == s), key=lambda b: (-abs(b[0]) - abs(b[1]), b)) for s in range(count + 1)]


def ways(trees):
    groups = {(0, ""): []}
    for part, (parent, stages) in enumerate(trees):
        below = {}
        for block, up in parent.items():
            below.setdefault(up, []).append(block)

        def depth(block):
            return 1 + max([depth(b) for b in below.get(block, [])], default=0)

        for s, blocks in enumerate(stages):
            for block in blocks:
                came = ""
                if s:
                    dy, dz = wrap(parent[block][0] - block[0], NY), wrap(parent[block][1] - block[1], NZ)
                    came = ("y+" if dy > 0 else "y-") if dy else ("z+" if dz > 0 else "z-")
                    if dy == NY // 2:
                        came = "y2"
                nexts = sorted(below.get(block, []), key=lambda b: (-depth(b), b))
                groups.setdefault((s, came), []).append((part, block, nexts))
    keys = sorted(groups)
    return [groups[k] for k in keys], keys


TOK_WAYS = [ways(t) for t in ((tree("y", "all", "two"), tree("z", "all", "two")), (tree("y", "all", "two"), tree("z", "all", "two")), (tree("y", "all", "two"), tree("z", "all", "two")), (tree("y", "all", "two"), tree("z", "all", "two")))]
HID_WAYS = [ways(t) for t in ((tree("y", None, None), tree("z", None, None)), (tree("y", None, None), tree("z", None, None)), (tree("y", None, None), tree("z", None, None)), (tree("y", "all", None), tree("z", "all", None)))]

SHIFTS = {
    (sign * (block[0] - after[0]) % NY, sign * (block[1] - after[1]) % NZ)
    for groups, _ in TOK_WAYS + HID_WAYS for group in groups for _, block, nexts in group for after in nexts for sign in (1, -1)
}
SHIFTS = sorted(SHIFTS)

ORDER = [
    ("tok", 0, 0), ("tok", 1, 0), ("tok", 0, 1), ("tok", 0, 2), ("tok", 0, 4), ("tok", 0, 5),
    ("tok", 0, 3), ("tok", 2, 0), ("tok", 1, 1), ("tok", 1, 2), ("tok", 1, 4), ("tok", 1, 5),
    ("tok", 1, 3), ("tok", 3, 0), ("tok", 0, 6), ("tok", 0, 7), ("tok", 0, 9), ("tok", 2, 1),
    ("tok", 0, 8), ("tok", 0, 10), ("tok", 2, 2), ("tok", 2, 4), ("tok", 2, 3), ("tok", 2, 5),
    ("tok", 1, 6), ("tok", 1, 7), ("tok", 3, 1), ("tok", 1, 8), ("tok", 1, 9), ("tok", 3, 2),
    ("tok", 3, 3), ("tok", 3, 4), ("tok", 1, 10), ("tok", 0, 11), ("tok", 0, 12), ("tok", 0, 14),
    ("tok", 3, 5), ("tok", 0, 13), ("tok", 2, 6), ("tok", 2, 7), ("tok", 0, 15), ("pack", 0, 0),
    ("tok", 2, 8), ("theirs", 0, 2), ("tok", 2, 9), ("theirs", 0, 1), ("theirs", 0, 3), ("theirs", 0, 0),
    ("tok", 1, 11), ("tok", 1, 12), ("tok", 1, 14), ("tok", 2, 10), ("tok", 1, 13), ("tok", 3, 6),
    ("tok", 3, 7), ("mine", 0, 2), ("mine", 0, 1), ("tok", 3, 8), ("tok", 3, 9), ("mine", 0, 3),
    ("mine", 0, 0), ("tok", 1, 15), ("pack", 1, 0), ("theirs", 1, 2), ("tok", 2, 14), ("theirs", 1, 1),
    ("theirs", 1, 3), ("theirs", 1, 0), ("tok", 3, 10), ("tok", 2, 11), ("tok", 2, 12), ("tok", 2, 15),
    ("mine", 1, 2), ("tok", 2, 13), ("pack", 2, 0), ("mine", 1, 1), ("theirs", 2, 2), ("tok", 3, 14),
    ("mine", 1, 3), ("theirs", 2, 1), ("mine", 1, 0), ("theirs", 2, 3), ("act", 0, 0), ("tok", 3, 11),
    ("tok", 3, 12), ("tok", 3, 15), ("theirs", 2, 0), ("mine", 2, 2), ("tok", 3, 13), ("mine", 2, 1),
    ("pack", 3, 0), ("mine", 2, 3), ("theirs", 3, 2), ("theirs", 3, 1), ("theirs", 3, 3), ("mine", 2, 0),
    ("theirs", 3, 0), ("hid", 0, 4), ("hid", 0, 3), ("act", 1, 0), ("hid", 0, 1), ("hid", 0, 2),
    ("mine", 3, 2), ("mine", 3, 1), ("mine", 3, 3), ("mine", 3, 0), ("act", 2, 0), ("hid", 0, 5),
    ("hid", 1, 3), ("hid", 1, 4), ("hid", 0, 7), ("hid", 0, 8), ("hid", 1, 1), ("hid", 1, 2),
    ("hid", 0, 6), ("hid", 2, 4), ("hid", 2, 3), ("act", 3, 0), ("hid", 2, 1), ("hid", 2, 2),
    ("hid", 0, 10), ("hid", 1, 5), ("hid", 1, 7), ("hid", 0, 11), ("hid", 0, 12), ("hid", 0, 9),
    ("hid", 1, 6), ("hid", 1, 8), ("hid", 2, 5), ("hid", 3, 4), ("hid", 3, 5), ("hid", 2, 8),
    ("hid", 2, 7), ("hid", 3, 1), ("hid", 3, 2), ("hid", 3, 3), ("hid", 2, 6), ("hid", 0, 16),
    ("hid", 0, 15), ("hid", 1, 11), ("hid", 0, 13), ("hid", 1, 9), ("hid", 0, 14), ("hid", 1, 12),
    ("hid", 1, 10), ("hid", 3, 9), ("hid", 2, 11), ("hid", 3, 6), ("hid", 3, 7), ("hid", 0, 19),
    ("hid", 3, 10), ("hid", 2, 10), ("hid", 2, 12), ("hid", 0, 20), ("hid", 0, 18), ("hid", 1, 15),
    ("hid", 2, 9), ("hid", 3, 8), ("hid", 1, 16), ("hid", 0, 17), ("hid", 1, 14), ("hid", 1, 13),
    ("hid", 3, 14), ("hid", 2, 15), ("hid", 3, 15), ("hid", 3, 12), ("hid", 1, 19), ("hid", 3, 11),
    ("hid", 2, 13), ("hid", 2, 16), ("hid", 3, 13), ("hid", 0, 22), ("hid", 2, 14), ("hid", 1, 20),
    ("hid", 3, 19), ("hid", 0, 21), ("mix", 0, 0), ("hid", 1, 17), ("hid", 1, 18), ("hid", 2, 19),
    ("hid", 3, 20), ("hid", 3, 16), ("hid", 3, 17), ("hid", 2, 20), ("hid", 1, 22), ("hid", 2, 18),
    ("hid", 3, 24), ("hid", 3, 18), ("scatter", 0, 0), ("hid", 2, 17), ("hid", 3, 25), ("hid", 1, 21),
    ("hid", 2, 22), ("mix", 1, 0), ("hid", 3, 21), ("hid", 3, 22), ("hid", 2, 21), ("hid", 3, 23),
    ("mix", 2, 0), ("mix", 3, 0), ("scatter", 1, 0), ("finish", 0, 0), ("scatter", 2, 0), ("scatter", 3, 0),
    ("finish", 1, 0), ("finish", 2, 0), ("finish", 3, 0),
]


def kernel(
    tok_hbm, gate_hbm, up_hbm, down_hbm, out_ref,
    tok, w1, wd, tok_all, lhs, own, part_out, part_in, sum_out, sum_in,
    hid_all, acc, acc_in, red_out, red_in,
    load_sem, tok_recv, hid_recv, part_recv, sum_recv, mix_recv, red_recv, send_sem,
):
    gx, gy = lax.axis_index("gx"), lax.axis_index("gy")
    x, core, y, z = gx // NC, gx % NC, gy // NZ, gy % NZ

    def at(dx=0, dc=0, dy=0, dz=0):
        return (
            (x + dx + NX) % NX * NC + (core + dc) % NC,
            (y + dy + NY) % NY * NZ + (z + dz + NZ) % NZ,
        )

    def remote(src, dst, sent, received, device):
        return pltpu.make_async_remote_copy(
            src_ref=src, dst_ref=dst, send_sem=sent, recv_sem=received, device_id=device, device_id_type=MESH
        )

    tok_load = pltpu.make_async_copy(tok_hbm, tok, load_sem.at[0])
    tok_load.start()
    barrier = pltpu.get_barrier_semaphore()
    peers = [at(dy=dy, dz=dz) for dy, dz in SHIFTS] + [at(dx=d) for d in (1, 2, 3)] + [at(dc=1)]
    for peer in peers:
        pl.semaphore_signal(barrier, inc=1, device_id=peer, device_id_type=MESH)

    w_wait = {}
    for i in (2, 1, 3, 0, 6, 5, 7, 4):
        share = (x + i % 4) % NX * NC + (core + 1 - i // 4) % NC
        columns = pl.ds(pl.multiple_of(share * 128, 128), 128)
        for h, src in enumerate((gate_hbm, up_hbm)):
            pltpu.make_async_copy(src.at[:, columns], w1.at[i, :, pl.ds(h * 128, 128)], load_sem.at[2 + i]).start()
        w_wait[i] = pltpu.make_async_copy(w1.at[i], w1.at[i], load_sem.at[2 + i])
    wd_load = pltpu.make_async_copy(down_hbm, wd, load_sem.at[1])
    wd_load.start()

    tok_load.wait()
    turned = jnp.swapaxes(tok[...], 0, 1)
    for ch in range(CHUNKS):
        side = []
        for c in range(NC):
            side.append(jnp.concatenate(
                [turned[(i * NC + c) * 64 + ch * 16:(i * NC + c) * 64 + ch * 16 + 16, :] for i in range(NX)], axis=0
            ))
        tok_all[ch, pl.ds(pl.multiple_of(gy * HALF, HALF), HALF)] = jnp.concatenate(side, axis=1)
    pl.semaphore_wait(barrier, len(peers))

    unsent = {}

    def flush(k):
        for copy in unsent.pop(k, ()):
            copy.wait_send()

    class Gather:
        def __init__(self, ref, ch, ways, cut, size, received, k):
            self.ref, self.ch, self.size, self.received, self.k = ref, ch, size, received, k
            self.groups, self.keys = ways
            self.parts = ((0, cut), (cut, size - cut))
            unsent[k] = [self.rows_of((NY * NZ - 1) * size, 0)]

        def rows_of(self, count, g):
            rows = self.ref.at[self.ch, pl.ds(0, count)]
            return remote(rows, rows, send_sem.at[self.k], self.received.at[self.ch, g], at(dy=1))

        def step(self, g):
            group = self.groups[g]
            if g > 0:
                self.rows_of(sum(self.parts[part][1] for part, _, _ in group), g - 1).wait_recv()
            moves = []
            for part, block, nexts in group:
                slot = (y + block[0] + NY) % NY * NZ + (z + block[1] + NZ) % NZ
                first, count = self.parts[part]
                rows = self.ref.at[self.ch, pl.ds(pl.multiple_of(slot * self.size + first, 16), count)]
                for after in nexts:
                    dy, dz = wrap(block[0] - after[0], NY), wrap(block[1] - after[1], NZ)
                    moves.append((rows, at(dy=dy, dz=dz), self.arrives(part, after)))
            for rows, device, there in moves:
                remote(rows, rows, send_sem.at[self.k], self.received.at[self.ch, there - 1], device).start()

        def arrives(self, part, block):
            for g, group in enumerate(self.groups):
                if any(p == part and b == block for p, b, _ in group):
                    return g

    tok_gather = [Gather(tok_all, ch, TOK_WAYS[ch], TOK_CUTS[ch], HALF, tok_recv, ch) for ch in range(CHUNKS)]
    hid_gather = [Gather(hid_all, ch, HID_WAYS[ch], HID_CUTS[ch], ROWS, hid_recv, CHUNKS + ch) for ch in range(CHUNKS)]

    def send_parts(ch, i):
        return remote(part_out.at[ch, i], part_in.at[ch, i], send_sem.at[2 * CHUNKS + ch], part_recv.at[ch, i], at(dc=1))

    def send_sum(ch, i):
        k = 3 * CHUNKS + ch
        return remote(sum_out.at[ch, i - 1], sum_in.at[ch, i - 1], send_sem.at[k], sum_recv.at[ch], at(dx=i))

    def tok_step(ch, s):
        tok_gather[ch].step(s)

    def pack(ch, _):
        for a in range(0, NY * NZ, 2):
            lo, hi = tok_all[ch, a * HALF:(a + 1) * HALF], tok_all[ch, (a + 1) * HALF:(a + 2) * HALF]
            columns = slice(a * 64, a * 64 + 128)
            lhs[ch % 2, :HALF, columns] = jnp.concatenate([lo[:, :64], hi[:, :64]], axis=1)
            lhs[ch % 2, HALF:, columns] = jnp.concatenate([lo[:, 64:], hi[:, 64:]], axis=1)

    def theirs(ch, i):
        if ch == 0:
            w_wait[i].wait()
        part_out[ch, i] = jnp.dot(lhs[ch % 2], w1[i], preferred_element_type=jnp.float32)
        send_parts(ch, i).start()
        if i == 0:
            unsent[2 * CHUNKS + ch] = [remote(part_out.at[ch], part_in.at[ch], send_sem.at[2 * CHUNKS + ch], part_recv.at[ch, i], at(dc=1))]

    def mine(ch, i):
        if ch == 0:
            w_wait[4 + i].wait()
        total = jnp.dot(lhs[ch % 2], w1[4 + i], preferred_element_type=jnp.float32)
        send_parts(ch, i).wait_recv()
        total = total + part_in[ch, i]
        if i == 0:
            own[ch] = total
        else:
            sum_out[ch, i - 1] = total.astype(jnp.bfloat16)
            send_sum(ch, i).start()

    def activate(ch, _):
        k = 3 * CHUNKS + ch
        sums = remote(sum_out.at[ch], sum_in.at[ch], send_sem.at[k], sum_recv.at[ch], at(dx=1))
        unsent[k] = [sums]
        sums.wait_recv()
        total = own[ch]
        for i in range(3):
            total = total + sum_in[ch, i].astype(jnp.float32)
        gate, up = total[:, :128], total[:, 128:]
        hid_all[ch, pl.ds(pl.multiple_of(gy * ROWS, ROWS), ROWS)] = (gate / (1.0 + jnp.exp(-gate)) * up).astype(jnp.bfloat16)
        hid_gather[ch].step(0)

    def hid_step(ch, s):
        hid_gather[ch].step(s)

    def mix(ch, _):
        if ch == 0:
            wd_load.wait()
        rows = jnp.concatenate([hid_all[ch, a * ROWS:(a + 1) * ROWS] for a in range(NY * NZ)], axis=1)
        acc[ch] = jnp.dot(rows, wd[...].reshape(NY * NZ * 128, 512), preferred_element_type=jnp.float32)
        mixed_parts(ch).start()
        unsent[4 * CHUNKS + ch] = [mixed_parts(ch)]

    def mixed_parts(ch):
        part = pl.ds(pl.multiple_of((1 - core) * HALF, HALF), HALF)
        return remote(acc.at[ch, part], acc_in.at[ch], send_sem.at[4 * CHUNKS + ch], mix_recv.at[ch], at(dc=1))

    def scatter(ch, _):
        mixed_parts(ch).wait_recv()
        for i in (2, 1, 3, 0):
            place = (x + i) % NX * 16
            rows = pl.ds(pl.multiple_of(core * HALF + place, 16), 16)
            total = acc[ch, rows, :] + acc_in[ch, pl.ds(pl.multiple_of(place, 16), 16), :]
            if i == 0:
                red_own[ch] = total
            else:
                red_out[ch, i - 1] = total.astype(jnp.bfloat16)
                remote(red_out.at[ch, i - 1], red_in.at[ch, i - 1], send_sem.at[5 * CHUNKS + ch], red_recv.at[ch], at(dx=i)).start()

    red_own = {}

    def finish(ch, _):
        k = 5 * CHUNKS + ch
        parts = remote(red_out.at[ch], red_in.at[ch], send_sem.at[k], red_recv.at[ch], at(dx=1))
        unsent[k] = [parts]
        parts.wait_recv()
        total = red_own[ch]
        for i in range(3):
            total = total + red_in[ch, i].astype(jnp.float32)
        out_ref[ch * 16:(ch + 1) * 16, :] = total.astype(jnp.bfloat16)

    actions = {
        "tok": tok_step, "pack": pack, "theirs": theirs, "mine": mine, "act": activate, "hid": hid_step,
        "mix": mix, "scatter": scatter, "finish": finish,
    }
    for name, ch, step in ORDER:
        actions[name](ch, step)

    for k in list(unsent):
        flush(k)


def body(tokens, gate_weight, up_weight, down_weight):
    bf16, f32 = jnp.bfloat16, jnp.float32
    return pl.pallas_call(
        kernel,
        out_shape=jax.ShapeDtypeStruct((64, 512), bf16),
        in_specs=[pl.BlockSpec(memory_space=pl.ANY)] * 4,
        out_specs=pl.BlockSpec(memory_space=pltpu.VMEM),
        scratch_shapes=[
            pltpu.VMEM((64, 512), bf16),
            pltpu.VMEM((8, 2048, 256), bf16),
            pltpu.VMEM((32, 128, 512), bf16),
            pltpu.VMEM((CHUNKS, NY * NZ * HALF, 128), bf16),
            pltpu.VMEM((2, ROWS, 2048), bf16),
            pltpu.VMEM((CHUNKS, ROWS, 256), f32),
            pltpu.VMEM((CHUNKS, 4, ROWS, 256), f32),
            pltpu.VMEM((CHUNKS, 4, ROWS, 256), f32),
            pltpu.VMEM((CHUNKS, 3, ROWS, 256), bf16),
            pltpu.VMEM((CHUNKS, 3, ROWS, 256), bf16),
            pltpu.VMEM((CHUNKS, NY * NZ * ROWS, 128), bf16),
            pltpu.VMEM((CHUNKS, ROWS, 512), f32),
            pltpu.VMEM((CHUNKS, HALF, 512), f32),
            pltpu.VMEM((CHUNKS, 3, 16, 512), bf16),
            pltpu.VMEM((CHUNKS, 3, 16, 512), bf16),
            pltpu.SemaphoreType.DMA((10,)),
            pltpu.SemaphoreType.DMA((CHUNKS, max(len(w[0]) for w in TOK_WAYS) - 1)),
            pltpu.SemaphoreType.DMA((CHUNKS, max(len(w[0]) for w in HID_WAYS) - 1)),
            pltpu.SemaphoreType.DMA((CHUNKS, 4)),
            pltpu.SemaphoreType.DMA((CHUNKS,)),
            pltpu.SemaphoreType.DMA((CHUNKS,)),
            pltpu.SemaphoreType.DMA((CHUNKS,)),
            pltpu.SemaphoreType.DMA((6 * CHUNKS,)),
        ],
        compiler_params=pltpu.CompilerParams(
            collective_id=0, has_side_effects=True, vmem_limit_bytes=56 * 1024 * 1024
        ),
        cost_estimate=pl.CostEstimate(flops=6442450944, bytes_accessed=12 << 20, transcendentals=0),
    )(tokens.T, gate_weight, up_weight, down_weight)


def solution(mesh):
    in_specs = (P(None, ("gx", "gy")), P("gx", "gy"), P("gx", "gy"), P(None, "gx", "gy"))
    return jax.shard_map(body, mesh=mesh, in_specs=in_specs, out_specs=P("gx", "gy"), check_vma=False)
```

```python
import jax
import jax.numpy as jnp
from jax import lax
from jax.experimental import pallas as pl
from jax.experimental.pallas import tpu as pltpu
from jax.sharding import PartitionSpec as P

MESH = pl.DeviceIdType.MESH
NX, NC, NY, NZ = 4, 2, 4, 8
CHUNKS = 4
ROWS = 128
HALF = ROWS // 2
TOK_CUTS = (16, 16, 32, 16)
HID_CUTS = (32, 48, 32, 64)


def wrap(d, n):
    d %= n
    return d - n if d > n // 2 else d


def place(i):
    return wrap(i // NZ, NY), wrap(i % NZ, NZ)


def tree(parents):
    parent = {place(i): place(up) for i, up in enumerate(parents) if i}
    stage = {(0, 0): 0}

    def visit(block):
        if block not in stage:
            stage[block] = visit(parent[block]) + 1
        return stage[block]

    for block in parent:
        visit(block)
    return parent, [[block for block in stage if stage[block] == s] for s in range(max(stage.values()) + 1)]


def depth_of(parent, block):
    return 1 + max([depth_of(parent, b) for b, up in parent.items() if up == block], default=0)


def ways(trees):
    groups = {(0, ""): []}
    for part, (parent, stages) in enumerate(trees):
        below = {}
        for block, up in parent.items():
            below.setdefault(up, []).append(block)

        for s, blocks in enumerate(stages):
            for block in blocks:
                came = ""
                if s:
                    dy, dz = wrap(parent[block][0] - block[0], NY), wrap(parent[block][1] - block[1], NZ)
                    came = ("y+" if dy > 0 else "y-") if dy else ("z+" if dz > 0 else "z-")
                    if dy == NY // 2:
                        came = "y2"
                nexts = sorted(below.get(block, []), key=lambda b: (-depth_of(parent, b), b))
                groups.setdefault((s, came), []).append((part, block, nexts))
    keys = sorted(groups)
    return [groups[k] for k in keys], [parent for parent, _ in trees]


PARENTS = (
    (0, 0, 0, 2, 2, 6, 0, 0, 0, 1, 8, 9, 15, 5, 6, 8, 0, 25, 10, 27, 21, 16, 30, 15, 0, 24, 24, 24, 27, 5, 24, 24),
    (0, 0, 0, 1, 6, 6, 0, 0, 0, 1, 2, 3, 4, 15, 6, 7, 24, 9, 2, 18, 4, 5, 16, 16, 0, 24, 2, 26, 4, 5, 31, 24),
    (0, 0, 0, 2, 1, 6, 0, 0, 0, 1, 8, 9, 4, 5, 15, 7, 24, 25, 10, 3, 16, 5, 30, 31, 0, 1, 2, 24, 4, 31, 6, 7),
    (0, 0, 0, 1, 2, 6, 0, 0, 0, 1, 2, 9, 14, 14, 6, 7, 0, 25, 2, 3, 4, 5, 30, 16, 0, 1, 2, 26, 4, 31, 6, 7),
    (0, 0, 0, 0, 2, 6, 7, 0, 0, 1, 9, 3, 10, 15, 6, 7, 8, 16, 16, 11, 4, 23, 6, 15, 0, 1, 25, 3, 27, 24, 31, 7),
    (0, 0, 0, 2, 1, 6, 0, 0, 0, 8, 8, 3, 4, 15, 6, 8, 8, 9, 16, 17, 4, 5, 14, 15, 0, 1, 2, 26, 30, 30, 24, 24),
    (0, 0, 0, 0, 1, 0, 0, 0, 0, 1, 8, 10, 4, 15, 15, 7, 24, 25, 2, 3, 19, 16, 16, 31, 0, 24, 24, 25, 24, 24, 31, 24),
    (0, 0, 0, 1, 2, 7, 0, 0, 0, 8, 2, 9, 4, 5, 6, 8, 8, 16, 2, 3, 4, 23, 14, 7, 0, 1, 2, 26, 4, 24, 31, 24),
    (0, 0, 0, 2, 2, 6, 0, 0, 0, 1, 2, 3, 4, 14, 8, 8, 0, 25, 10, 18, 4, 29, 14, 16, 0, 1, 2, 3, 26, 30, 6, 7),
    (0, 0, 0, 2, 2, 6, 0, 0, 0, 1, 2, 10, 4, 5, 6, 8, 0, 16, 10, 11, 12, 29, 6, 31, 0, 24, 2, 3, 4, 5, 6, 7),
    (0, 0, 0, 0, 3, 6, 0, 0, 0, 8, 2, 3, 11, 14, 15, 8, 0, 25, 10, 27, 12, 29, 14, 31, 0, 24, 2, 3, 4, 30, 31, 7),
    (0, 0, 1, 2, 5, 0, 7, 0, 0, 1, 9, 10, 11, 5, 8, 8, 0, 25, 26, 18, 28, 22, 14, 15, 0, 1, 25, 3, 4, 5, 31, 24),
    (0, 0, 1, 2, 5, 7, 7, 0, 0, 8, 9, 3, 4, 14, 15, 8, 8, 25, 17, 27, 28, 23, 23, 16, 0, 1, 24, 26, 26, 5, 6, 7),
    (0, 0, 0, 2, 2, 6, 7, 0, 0, 1, 2, 3, 4, 5, 6, 8, 8, 16, 10, 11, 28, 5, 14, 15, 0, 1, 25, 26, 4, 30, 31, 24),
    (0, 0, 1, 2, 5, 7, 7, 0, 0, 1, 2, 10, 13, 5, 15, 8, 8, 16, 26, 3, 17, 13, 23, 16, 0, 24, 2, 26, 29, 5, 31, 24),
    (0, 0, 0, 2, 2, 6, 0, 0, 0, 1, 2, 3, 4, 15, 15, 8, 24, 25, 10, 27, 12, 29, 30, 16, 0, 1, 2, 26, 27, 5, 6, 7),
)
TOK_WAYS = [ways([tree(PARENTS[i]) for i in pair]) for pair in ((0, 1), (2, 3), (4, 5), (6, 7))]
HID_WAYS = [ways([tree(PARENTS[i]) for i in pair]) for pair in ((8, 9), (10, 11), (12, 13), (14, 15))]

SHIFTS = {
    (sign * (block[0] - after[0]) % NY, sign * (block[1] - after[1]) % NZ)
    for groups, _ in TOK_WAYS + HID_WAYS for group in groups for _, block, nexts in group for after in nexts for sign in (1, -1)
}
SHIFTS = sorted(SHIFTS)

LHS = (0, 1, 0, 1)

ORDER = [
    ("tok", 0, 0), ("tok", 1, 0), ("tok", 2, 0), ("tok", 0, 1), ("tok", 0, 2), ("tok", 0, 3),
    ("tok", 0, 4), ("tok", 0, 5), ("tok", 1, 1), ("tok", 1, 2), ("tok", 1, 3), ("tok", 1, 4),
    ("tok", 1, 5), ("tok", 2, 1), ("tok", 2, 2), ("tok", 2, 3), ("tok", 2, 4), ("tok", 0, 6),
    ("tok", 0, 9), ("tok", 0, 7), ("tok", 0, 10), ("tok", 0, 8), ("tok", 1, 9), ("tok", 3, 0),
    ("tok", 1, 6), ("tok", 1, 7), ("tok", 1, 10), ("tok", 1, 8), ("tok", 2, 5), ("tok", 2, 7),
    ("tok", 2, 6), ("tok", 0, 15), ("tok", 2, 8), ("tok", 0, 11), ("tok", 0, 12), ("tok", 0, 13),
    ("tok", 0, 14), ("pack", 0, 0), ("theirs", 0, 2), ("tok", 3, 1), ("tok", 3, 2), ("tok", 1, 12),
    ("theirs", 0, 1), ("tok", 3, 4), ("theirs", 0, 3), ("tok", 3, 3), ("theirs", 0, 0), ("tok", 1, 11),
    ("tok", 1, 15), ("mine", 0, 2), ("tok", 1, 13), ("tok", 1, 14), ("pack", 1, 0), ("theirs", 1, 2),
    ("mine", 0, 1), ("tok", 2, 9), ("mine", 0, 3), ("tok", 2, 12), ("theirs", 1, 1), ("mine", 0, 0),
    ("tok", 2, 10), ("theirs", 1, 3), ("tok", 2, 11), ("theirs", 1, 0), ("tok", 3, 5), ("mine", 1, 2),
    ("tok", 3, 6), ("tok", 3, 9), ("mine", 1, 1), ("mine", 1, 3), ("tok", 3, 7), ("tok", 3, 8),
    ("mine", 1, 0), ("tok", 2, 13), ("tok", 2, 14), ("pack", 2, 0), ("theirs", 2, 2), ("theirs", 2, 1),
    ("theirs", 2, 3), ("theirs", 2, 0), ("act", 0, 0), ("mine", 2, 2), ("tok", 3, 10), ("tok", 3, 14),
    ("tok", 3, 11), ("mine", 2, 1), ("tok", 3, 12), ("tok", 3, 13), ("pack", 3, 0), ("mine", 2, 3),
    ("act", 1, 0), ("mine", 2, 0), ("theirs", 3, 2), ("theirs", 3, 1), ("theirs", 3, 3), ("hid", 0, 2),
    ("theirs", 3, 0), ("hid", 0, 5), ("hid", 0, 1), ("hid", 0, 4), ("hid", 0, 3), ("mine", 3, 2),
    ("mine", 3, 1), ("hid", 1, 2), ("hid", 1, 1), ("mine", 3, 3), ("act", 2, 0), ("mine", 3, 0),
    ("hid", 1, 5), ("hid", 1, 3), ("hid", 1, 4), ("hid", 0, 7), ("hid", 0, 9), ("hid", 0, 10),
    ("hid", 0, 6), ("hid", 0, 8), ("hid", 2, 2), ("hid", 2, 1), ("act", 3, 0), ("hid", 2, 3),
    ("hid", 1, 7), ("hid", 1, 6), ("hid", 2, 4), ("hid", 1, 8), ("hid", 1, 9), ("hid", 0, 14),
    ("hid", 0, 12), ("hid", 0, 15), ("hid", 0, 11), ("hid", 0, 13), ("hid", 3, 1), ("hid", 3, 2),
    ("hid", 3, 4), ("hid", 3, 3), ("hid", 2, 7), ("hid", 2, 6), ("hid", 2, 5), ("hid", 1, 12),
    ("hid", 1, 11), ("hid", 1, 10), ("hid", 1, 13), ("hid", 0, 17), ("hid", 0, 18), ("hid", 0, 16),
    ("hid", 2, 8), ("mix", 0, 0), ("hid", 3, 6), ("hid", 3, 7), ("hid", 3, 5), ("hid", 3, 8),
    ("hid", 2, 11), ("hid", 1, 17), ("hid", 1, 15), ("hid", 1, 14), ("hid", 1, 16), ("hid", 2, 9),
    ("hid", 2, 10), ("hid", 2, 12), ("hid", 3, 12), ("finish", 0, 0), ("hid", 3, 10), ("hid", 3, 9),
    ("hid", 1, 19), ("hid", 3, 11), ("hid", 1, 18), ("mix", 1, 0), ("hid", 2, 13), ("hid", 2, 15),
    ("hid", 2, 16), ("hid", 2, 17), ("hid", 2, 14), ("mix", 2, 0), ("hid", 3, 15), ("hid", 3, 16),
    ("hid", 3, 14), ("hid", 3, 17), ("hid", 3, 13), ("mix", 3, 0), ("finish", 1, 0), ("finish", 2, 0),
    ("finish", 3, 0),
]


def kernel(
    tok_hbm, gate_hbm, up_hbm, down_hbm, out_ref,
    tok, w1, wd, tok_all, lhs, own, part_out, part_in, sum_out, sum_in,
    hid_all, acc, red_out, red_in,
    load_sem, tok_recv, hid_recv, part_recv, sum_recv, red_recv, send_sem,
):
    gx, gy = lax.axis_index("gx"), lax.axis_index("gy")
    x, core, y, z = gx // NC, gx % NC, gy // NZ, gy % NZ

    xs = [(x + d) % NX * NC for d in range(NX)]
    cores = [core, 1 - core]
    ys = [(y + d) % NY * NZ for d in range(NY)]
    zs = [(z + d) % NZ for d in range(NZ)]
    places = {}

    def slot_of(dy, dz):
        key = (dy % NY, dz % NZ)
        if key not in places:
            places[key] = ys[key[0]] + zs[key[1]] if any(key) else gy
        return places[key]

    def at(dx=0, dc=0, dy=0, dz=0):
        return (xs[dx % NX] + cores[dc % NC] if dx % NX or dc % NC else gx, slot_of(dy, dz))

    def remote(src, dst, sent, received, device):
        return pltpu.make_async_remote_copy(
            src_ref=src, dst_ref=dst, send_sem=sent, recv_sem=received, device_id=device, device_id_type=MESH
        )

    tok_load = pltpu.make_async_copy(tok_hbm, tok, load_sem.at[0])
    tok_load.start()
    barrier = pltpu.get_barrier_semaphore()
    peers = [at(dy=dy, dz=dz) for dy, dz in SHIFTS] + [at(dx=dx, dc=dc) for dx in range(NX) for dc in range(NC) if dx + dc]
    for peer in peers:
        pl.semaphore_signal(barrier, inc=1, device_id=peer, device_id_type=MESH)

    w_wait = {}
    for i in (2, 1, 3, 0, 6, 5, 7, 4):
        share = at(dx=i % 4, dc=1 - i // 4)[0]
        columns = pl.ds(pl.multiple_of(share * 128, 128), 128)
        for h, src in enumerate((gate_hbm, up_hbm)):
            pltpu.make_async_copy(src.at[:, columns], w1.at[i, :, pl.ds(h * 128, 128)], load_sem.at[2 + i]).start()
        w_wait[i] = pltpu.make_async_copy(w1.at[i], w1.at[i], load_sem.at[2 + i])
    wd_load = pltpu.make_async_copy(down_hbm, wd, load_sem.at[1])
    wd_load.start()

    tok_load.wait()
    turned = jnp.swapaxes(tok[...], 0, 1)
    for ch in range(CHUNKS):
        side = []
        for c in range(NC):
            side.append(jnp.concatenate(
                [turned[(i * NC + c) * 64 + ch * 16:(i * NC + c) * 64 + ch * 16 + 16, :] for i in range(NX)], axis=0
            ))
        tok_all[ch, pl.ds(pl.multiple_of(gy * HALF, HALF), HALF)] = jnp.concatenate(side, axis=1)
    pl.semaphore_wait(barrier, len(peers))

    unsent = {}

    def flush(k):
        for copy in unsent.pop(k, ()):
            copy.wait_send()

    class Gather:
        def __init__(self, ref, ch, ways, cut, size, received, k):
            self.ref, self.ch, self.size, self.received, self.k = ref, ch, size, received, k
            self.groups, self.trees = ways
            self.parts = ((0, cut), (cut, size - cut))

        def rows_of(self, count, g):
            rows = self.ref.at[self.ch, pl.ds(0, count)]
            return remote(rows, rows, send_sem.at[self.k], self.received.at[self.ch, g], at(dy=1))

        def step(self, g):
            group = self.groups[g]
            if g == 0:
                unsent[self.k] = [self.rows_of((NY * NZ - 1) * self.size, 0)]
            else:
                self.rows_of(sum(self.parts[part][1] for part, _, _ in group), g - 1).wait_recv()
            moves = []
            for part, block, nexts in group:
                slot = slot_of(*block)
                first, count = self.parts[part]
                rows = self.ref.at[self.ch, pl.ds(pl.multiple_of(slot * self.size + first, 16), count)]
                for after in nexts:
                    dy, dz = wrap(block[0] - after[0], NY), wrap(block[1] - after[1], NZ)
                    moves.append((-depth_of(self.trees[part], after), rows, at(dy=dy, dz=dz), self.arrives(part, after)))
            moves.sort(key=lambda move: move[0])
            for _, rows, device, there in moves:
                remote(rows, rows, send_sem.at[self.k], self.received.at[self.ch, there - 1], device).start()

        def arrives(self, part, block):
            for g, group in enumerate(self.groups):
                if any(p == part and b == block for p, b, _ in group):
                    return g

    tok_gather = [Gather(tok_all, ch, TOK_WAYS[ch], TOK_CUTS[ch], HALF, tok_recv, ch) for ch in range(CHUNKS)]
    hid_gather = [Gather(hid_all, ch, HID_WAYS[ch], HID_CUTS[ch], ROWS, hid_recv, CHUNKS + ch) for ch in range(CHUNKS)]

    def send_parts(ch, i):
        return remote(part_out.at[ch, i], part_in.at[ch, i], send_sem.at[2 * CHUNKS + ch], part_recv.at[ch, i], at(dc=1))

    def send_sum(ch, i):
        k = 3 * CHUNKS + ch
        return remote(sum_out.at[ch, i - 1], sum_in.at[ch, i - 1], send_sem.at[k], sum_recv.at[ch], at(dx=i))

    def tok_step(ch, s):
        tok_gather[ch].step(s)

    def pack(ch, _):
        for a in range(0, NY * NZ, 2):
            lo, hi = tok_all[ch, a * HALF:(a + 1) * HALF], tok_all[ch, (a + 1) * HALF:(a + 2) * HALF]
            columns = slice(a * 64, a * 64 + 128)
            lhs[LHS[ch], :HALF, columns] = jnp.concatenate([lo[:, :64], hi[:, :64]], axis=1)
            lhs[LHS[ch], HALF:, columns] = jnp.concatenate([lo[:, 64:], hi[:, 64:]], axis=1)

    def theirs(ch, i):
        if ch == 0:
            w_wait[i].wait()
        part_out[ch, i] = jnp.dot(lhs[LHS[ch]], w1[i], preferred_element_type=jnp.float32)
        send_parts(ch, i).start()
        if i == 0:
            unsent[2 * CHUNKS + ch] = [remote(part_out.at[ch], part_in.at[ch], send_sem.at[2 * CHUNKS + ch], part_recv.at[ch, i], at(dc=1))]

    def mine(ch, i):
        if ch == 0:
            w_wait[4 + i].wait()
        total = jnp.dot(lhs[LHS[ch]], w1[4 + i], preferred_element_type=jnp.float32)
        send_parts(ch, i).wait_recv()
        total = total + part_in[ch, i]
        if i == 0:
            own[ch] = total
        else:
            sum_out[ch, i - 1] = total.astype(jnp.bfloat16)
            send_sum(ch, i).start()

    def activate(ch, _):
        k = 3 * CHUNKS + ch
        sums = remote(sum_out.at[ch], sum_in.at[ch], send_sem.at[k], sum_recv.at[ch], at(dx=1))
        unsent[k] = [sums]
        sums.wait_recv()
        total = own[ch]
        for i in range(3):
            total = total + sum_in[ch, i].astype(jnp.float32)
        gate, up = total[:, :128], total[:, 128:]
        hid_all[ch, pl.ds(pl.multiple_of(gy * ROWS, ROWS), ROWS)] = (gate / (1.0 + jnp.exp(-gate)) * up).astype(jnp.bfloat16)
        hid_gather[ch].step(0)

    def hid_step(ch, s):
        hid_gather[ch].step(s)

    def mix(ch, _):
        if ch == 0:
            wd_load.wait()
        rows = jnp.concatenate([hid_all[ch, a * ROWS:(a + 1) * ROWS] for a in range(NY * NZ)], axis=1)
        total = jnp.dot(rows, wd[...].reshape(NY * NZ * 128, 512), preferred_element_type=jnp.float32)
        acc[ch] = total
        red_out[ch] = total.astype(jnp.bfloat16)
        for k, (dx, dc) in enumerate(((2, 0), (2, 1), (1, 0), (1, 1), (3, 0), (3, 1), (0, 1))):
            place = (core + dc) % NC * HALF + (x + dx) % NX * 16
            part = red_out.at[ch, pl.ds(pl.multiple_of(place, 16), 16)]
            there = red_in.at[ch, pl.ds(k * 16, 16)]
            remote(part, there, send_sem.at[4 * CHUNKS + ch], red_recv.at[ch], at(dx=dx, dc=dc)).start()
        unsent[4 * CHUNKS + ch] = [all_reduced(ch)]

    def all_reduced(ch):
        return remote(red_out.at[ch, pl.ds(0, 7 * 16)], red_in.at[ch], send_sem.at[4 * CHUNKS + ch], red_recv.at[ch], at(dc=1))

    def finish(ch, _):
        all_reduced(ch).wait_recv()
        total = acc[ch, pl.ds(pl.multiple_of(core * HALF + x * 16, 16), 16), :]
        for k in range(7):
            total = total + red_in[ch, k * 16:(k + 1) * 16].astype(jnp.float32)
        out_ref[ch * 16:(ch + 1) * 16, :] = total.astype(jnp.bfloat16)

    actions = {
        "tok": tok_step, "pack": pack, "theirs": theirs, "mine": mine, "act": activate, "hid": hid_step,
        "mix": mix, "finish": finish,
    }
    for name, ch, step in ORDER:
        actions[name](ch, step)

    for k in list(unsent):
        flush(k)


def body(tokens, gate_weight, up_weight, down_weight):
    bf16, f32 = jnp.bfloat16, jnp.float32
    return pl.pallas_call(
        kernel,
        out_shape=pltpu.VMEM((64, 512), bf16),
        in_specs=[pl.BlockSpec(memory_space=pl.ANY)] * 4,
        out_specs=pl.BlockSpec(memory_space=pltpu.VMEM),
        scratch_shapes=[
            pltpu.VMEM((64, 512), bf16),
            pltpu.VMEM((8, 2048, 256), bf16),
            pltpu.VMEM((32, 128, 512), bf16),
            pltpu.VMEM((CHUNKS, NY * NZ * HALF, 128), bf16),
            pltpu.VMEM((2, ROWS, 2048), bf16),
            pltpu.VMEM((CHUNKS, ROWS, 256), f32),
            pltpu.VMEM((CHUNKS, 4, ROWS, 256), f32),
            pltpu.VMEM((CHUNKS, 4, ROWS, 256), f32),
            pltpu.VMEM((CHUNKS, 3, ROWS, 256), bf16),
            pltpu.VMEM((CHUNKS, 3, ROWS, 256), bf16),
            pltpu.VMEM((CHUNKS, NY * NZ * ROWS, 128), bf16),
            pltpu.VMEM((CHUNKS, ROWS, 512), f32),
            pltpu.VMEM((CHUNKS, ROWS, 512), bf16),
            pltpu.VMEM((CHUNKS, 7 * 16, 512), bf16),
            pltpu.SemaphoreType.DMA((10,)),
            pltpu.SemaphoreType.DMA((CHUNKS, max(len(w[0]) for w in TOK_WAYS) - 1)),
            pltpu.SemaphoreType.DMA((CHUNKS, max(len(w[0]) for w in HID_WAYS) - 1)),
            pltpu.SemaphoreType.DMA((CHUNKS, 4)),
            pltpu.SemaphoreType.DMA((CHUNKS,)),
            pltpu.SemaphoreType.DMA((CHUNKS,)),
            pltpu.SemaphoreType.DMA((5 * CHUNKS,)),
        ],
        compiler_params=pltpu.CompilerParams(
            collective_id=0, has_side_effects=True, vmem_limit_bytes=56 * 1024 * 1024
        ),
        cost_estimate=pl.CostEstimate(flops=6442450944, bytes_accessed=12 << 20, transcendentals=0),
    )(tokens.T, gate_weight, up_weight, down_weight)


def solution(mesh):
    in_specs = (P(None, ("gx", "gy")), P("gx", "gy"), P("gx", "gy"), P(None, "gx", "gy"))
    return jax.shard_map(body, mesh=mesh, in_specs=in_specs, out_specs=P("gx", "gy"), check_vma=False)
```

```python
import jax
import jax.numpy as jnp
from jax import lax
from jax.experimental import pallas as pl
from jax.experimental.pallas import tpu as pltpu
from jax.sharding import PartitionSpec as P

MESH = pl.DeviceIdType.MESH
NX, NC, NY, NZ = 4, 2, 4, 8
CHUNKS = 4
ROWS = 128
HALF = ROWS // 2
TOK_CUTS = (16, 16, 48, 48)
HID_CUTS = (32, 32, 32, 80)


def wrap(d, n):
    d %= n
    return d - n if d > n // 2 else d


def place(i):
    return wrap(i // NZ, NY), wrap(i % NZ, NZ)


def tree(parents):
    parent = {place(i): place(up) for i, up in enumerate(parents) if i}
    stage = {(0, 0): 0}

    def visit(block):
        if block not in stage:
            stage[block] = visit(parent[block]) + 1
        return stage[block]

    for block in parent:
        visit(block)
    return parent, [[block for block in stage if stage[block] == s] for s in range(max(stage.values()) + 1)]


def depth_of(parent, block):
    return 1 + max([depth_of(parent, b) for b, up in parent.items() if up == block], default=0)


def ways(trees):
    groups = {(0, ""): []}
    for part, (parent, stages) in enumerate(trees):
        below = {}
        for block, up in parent.items():
            below.setdefault(up, []).append(block)

        for s, blocks in enumerate(stages):
            for block in blocks:
                came = ""
                if s:
                    dy, dz = wrap(parent[block][0] - block[0], NY), wrap(parent[block][1] - block[1], NZ)
                    came = ("y+" if dy > 0 else "y-") if dy else ("z+" if dz > 0 else "z-")
                    if dy == NY // 2:
                        came = "y2"
                nexts = sorted(below.get(block, []), key=lambda b: (-depth_of(parent, b), b))
                groups.setdefault((s, came), []).append((part, block, nexts))
    keys = sorted(groups)
    return [groups[k] for k in keys], [parent for parent, _ in trees]


PARENTS = (
    (0, 0, 0, 2, 6, 6, 0, 0, 0, 8, 2, 8, 10, 8, 6, 8, 8, 1, 2, 18, 4, 29, 30, 15, 0, 1, 2, 26, 4, 24, 6, 7),
    (0, 0, 0, 2, 2, 6, 0, 0, 0, 1, 2, 10, 4, 14, 8, 7, 8, 16, 26, 3, 4, 22, 6, 15, 0, 24, 2, 26, 26, 30, 6, 7),
    (0, 0, 0, 0, 6, 6, 0, 0, 0, 1, 8, 10, 4, 14, 6, 8, 0, 25, 16, 18, 18, 5, 30, 16, 0, 1, 2, 3, 25, 31, 6, 7),
    (0, 0, 0, 1, 2, 6, 0, 0, 0, 1, 9, 3, 4, 5, 8, 7, 0, 9, 26, 3, 4, 22, 6, 15, 0, 1, 2, 3, 30, 5, 6, 7),
    (0, 0, 0, 2, 5, 7, 0, 0, 0, 1, 9, 3, 4, 14, 6, 8, 8, 25, 2, 11, 12, 13, 23, 15, 0, 1, 25, 25, 26, 30, 6, 7),
    (0, 0, 1, 1, 1, 0, 0, 0, 0, 1, 2, 10, 14, 5, 15, 7, 24, 9, 10, 11, 17, 23, 16, 16, 0, 1, 2, 26, 26, 30, 24, 24),
    (0, 0, 0, 2, 6, 6, 0, 0, 0, 8, 2, 3, 9, 15, 15, 7, 8, 9, 26, 3, 22, 22, 6, 15, 0, 1, 2, 3, 4, 24, 31, 7),
    (0, 0, 0, 2, 1, 7, 0, 0, 0, 1, 8, 10, 15, 5, 6, 8, 0, 16, 10, 17, 22, 22, 16, 15, 0, 24, 2, 3, 25, 30, 6, 7),
    (0, 0, 1, 2, 2, 6, 0, 0, 0, 8, 8, 10, 14, 15, 6, 8, 24, 9, 2, 11, 18, 22, 16, 15, 0, 1, 2, 3, 4, 30, 24, 24),
    (0, 0, 0, 0, 6, 6, 0, 0, 0, 8, 2, 9, 11, 5, 15, 7, 0, 16, 2, 3, 19, 22, 6, 15, 0, 24, 2, 3, 4, 30, 6, 7),
    (0, 0, 1, 1, 3, 6, 7, 0, 0, 1, 9, 10, 4, 5, 8, 8, 24, 9, 26, 18, 18, 13, 23, 15, 0, 24, 25, 26, 27, 30, 31, 24),
    (0, 0, 1, 2, 3, 6, 7, 0, 0, 1, 2, 10, 4, 5, 15, 7, 8, 25, 10, 18, 4, 22, 30, 31, 0, 1, 2, 3, 29, 30, 6, 7),
    (0, 0, 1, 2, 5, 6, 0, 0, 0, 8, 2, 9, 14, 5, 6, 8, 0, 25, 17, 11, 21, 5, 30, 31, 0, 24, 2, 26, 4, 30, 31, 24),
    (0, 0, 1, 2, 5, 6, 0, 0, 0, 8, 2, 3, 13, 14, 6, 7, 8, 16, 26, 17, 22, 13, 14, 31, 0, 1, 2, 26, 4, 30, 6, 7),
    (0, 0, 1, 0, 5, 6, 7, 0, 0, 1, 2, 3, 10, 14, 6, 7, 8, 25, 10, 11, 28, 5, 23, 16, 0, 1, 25, 3, 27, 5, 6, 7),
    (0, 0, 1, 2, 5, 6, 0, 0, 0, 8, 2, 3, 4, 5, 6, 7, 24, 16, 10, 3, 17, 29, 30, 16, 0, 1, 2, 26, 4, 5, 31, 24),
)
TOK_WAYS = [ways([tree(PARENTS[i]) for i in pair]) for pair in ((0, 1), (2, 3), (4, 5), (6, 7))]
HID_WAYS = [ways([tree(PARENTS[i]) for i in pair]) for pair in ((8, 9), (10, 11), (12, 13), (14, 15))]

TOK_SEMS = [sum(len(w[0]) - 1 for w in TOK_WAYS[:ch]) for ch in range(CHUNKS + 1)]
HID_SEMS = [sum(len(w[0]) - 1 for w in HID_WAYS[:ch]) for ch in range(CHUNKS + 1)]
SHIFTS = {
    (sign * (block[0] - after[0]) % NY, sign * (block[1] - after[1]) % NZ)
    for groups, _ in TOK_WAYS + HID_WAYS for group in groups for _, block, nexts in group for after in nexts for sign in (1, -1)
}
SHIFTS = sorted(SHIFTS)

LHS = (0, 1, 0, 1)

ORDER = [
    ("tok", 0, 0), ("tok", 2, 0), ("tok", 1, 0), ("tok", 0, 2), ("tok", 0, 1), ("tok", 0, 4),
    ("tok", 0, 3), ("tok", 2, 1), ("tok", 2, 2), ("tok", 3, 0), ("tok", 2, 4), ("tok", 1, 2),
    ("tok", 1, 1), ("tok", 2, 3), ("tok", 1, 4), ("tok", 1, 3), ("tok", 1, 5), ("tok", 0, 9),
    ("tok", 0, 6), ("tok", 0, 8), ("tok", 0, 5), ("tok", 0, 7), ("tok", 3, 1), ("tok", 3, 2),
    ("tok", 3, 5), ("tok", 3, 3), ("tok", 3, 4), ("tok", 2, 6), ("tok", 2, 5), ("tok", 2, 7),
    ("tok", 2, 9), ("tok", 1, 7), ("tok", 2, 8), ("tok", 1, 8), ("tok", 1, 9), ("tok", 1, 10),
    ("tok", 0, 13), ("tok", 1, 6), ("tok", 0, 11), ("tok", 0, 10), ("tok", 0, 14), ("tok", 0, 12),
    ("pack", 0, 0), ("theirs", 0, 2), ("theirs", 0, 1), ("theirs", 0, 3), ("theirs", 0, 0), ("tok", 3, 7),
    ("tok", 3, 6), ("tok", 3, 8), ("tok", 3, 9), ("tok", 2, 10), ("tok", 2, 11), ("tok", 3, 10),
    ("mine", 0, 2), ("tok", 2, 12), ("tok", 2, 13), ("mine", 0, 1), ("tok", 1, 11), ("tok", 1, 12),
    ("mine", 0, 3), ("tok", 1, 14), ("tok", 1, 15), ("tok", 1, 13), ("pack", 1, 0), ("theirs", 1, 2),
    ("theirs", 1, 1), ("theirs", 1, 3), ("theirs", 1, 0), ("mine", 0, 0), ("tok", 3, 11), ("tok", 3, 12),
    ("mine", 1, 2), ("tok", 3, 13), ("tok", 2, 14), ("mine", 1, 1), ("tok", 3, 14), ("mine", 1, 3),
    ("tok", 2, 15), ("tok", 2, 16), ("tok", 3, 15), ("mine", 1, 0), ("pack", 3, 0), ("theirs", 3, 2),
    ("act", 0, 0), ("theirs", 3, 1), ("theirs", 3, 3), ("theirs", 3, 0), ("mine", 3, 2), ("tok", 2, 17),
    ("pack", 2, 0), ("theirs", 2, 2), ("theirs", 2, 1), ("theirs", 2, 3), ("theirs", 2, 0), ("mine", 3, 1),
    ("mine", 3, 3), ("act", 1, 0), ("hid", 0, 2), ("hid", 0, 1), ("mine", 2, 2), ("hid", 0, 4),
    ("hid", 0, 3), ("mine", 2, 1), ("mine", 2, 3), ("mine", 3, 0), ("hid", 0, 5), ("mine", 2, 0),
    ("hid", 1, 3), ("hid", 1, 4), ("hid", 1, 1), ("hid", 1, 2), ("act", 3, 0), ("hid", 0, 10),
    ("hid", 0, 9), ("hid", 0, 7), ("act", 2, 0), ("hid", 0, 8), ("hid", 1, 8), ("hid", 0, 6),
    ("hid", 1, 7), ("hid", 1, 6), ("hid", 3, 3), ("hid", 1, 5), ("hid", 3, 2), ("hid", 3, 1),
    ("hid", 3, 4), ("hid", 0, 13), ("hid", 0, 11), ("hid", 0, 12), ("hid", 2, 2), ("hid", 2, 1),
    ("hid", 2, 5), ("hid", 2, 4), ("hid", 0, 15), ("hid", 2, 3), ("hid", 1, 10), ("hid", 1, 12),
    ("hid", 0, 14), ("hid", 1, 9), ("hid", 3, 8), ("hid", 1, 11), ("hid", 3, 6), ("hid", 3, 5),
    ("hid", 3, 7), ("hid", 2, 9), ("hid", 2, 7), ("hid", 0, 19), ("hid", 0, 17), ("hid", 2, 8),
    ("hid", 0, 18), ("hid", 2, 6), ("hid", 0, 16), ("mix", 0, 0), ("hid", 1, 15), ("hid", 1, 13),
    ("hid", 1, 16), ("hid", 1, 14), ("hid", 3, 12), ("hid", 3, 11), ("hid", 3, 10), ("hid", 3, 9),
    ("hid", 2, 14), ("hid", 2, 11), ("hid", 2, 13), ("hid", 2, 10), ("hid", 2, 12), ("hid", 1, 20),
    ("finish", 0, 0), ("hid", 1, 19), ("hid", 1, 17), ("hid", 1, 18), ("mix", 1, 0), ("hid", 3, 15),
    ("hid", 3, 16), ("hid", 3, 13), ("hid", 3, 17), ("hid", 3, 14), ("mix", 3, 0), ("hid", 2, 17),
    ("hid", 2, 15), ("hid", 2, 16), ("hid", 2, 18), ("mix", 2, 0), ("finish", 1, 0), ("finish", 3, 0),
    ("finish", 2, 0),
]


def kernel(
    tok_hbm, gate_hbm, up_hbm, down_hbm, out_ref,
    tok, w1, wd, tok_all, lhs, own, part_out, part_in, sum_out, sum_in,
    hid_all, acc, red_out, red_in,
    load_sem, tok_recv, hid_recv, part_recv, sum_recv, red_recv, send_sem,
):
    gx, gy = lax.axis_index("gx"), lax.axis_index("gy")
    x, core, y, z = gx // NC, gx % NC, gy // NZ, gy % NZ

    xs = [(x + d) % NX * NC for d in range(NX)]
    cores = [core, 1 - core]
    ys = [(y + d) % NY * NZ for d in range(NY)]
    zs = [(z + d) % NZ for d in range(NZ)]
    places = {}

    def slot_of(dy, dz):
        key = (dy % NY, dz % NZ)
        if key not in places:
            places[key] = ys[key[0]] + zs[key[1]] if any(key) else gy
        return places[key]

    def at(dx=0, dc=0, dy=0, dz=0):
        return (xs[dx % NX] + cores[dc % NC] if dx % NX or dc % NC else gx, slot_of(dy, dz))

    def remote(src, dst, sent, received, device):
        return pltpu.make_async_remote_copy(
            src_ref=src, dst_ref=dst, send_sem=sent, recv_sem=received, device_id=device, device_id_type=MESH
        )

    barrier = pltpu.get_barrier_semaphore()
    peers = [at(dy=dy, dz=dz) for dy, dz in SHIFTS] + [at(dx=dx, dc=dc) for dx in range(NX) for dc in range(NC) if dx + dc]
    for peer in peers:
        pl.semaphore_signal(barrier, inc=1, device_id=peer, device_id_type=MESH)

    tok_load = pltpu.make_async_copy(tok_hbm, tok, load_sem.at[0])
    tok_load.start()
    w_wait = {}
    for i in (2, 1, 3, 0, 6, 5, 7, 4):
        share = at(dx=i % 4, dc=1 - i // 4)[0]
        columns = pl.ds(pl.multiple_of(share * 128, 128), 128)
        for h, src in enumerate((gate_hbm, up_hbm)):
            pltpu.make_async_copy(src.at[:, columns], w1.at[i, :, pl.ds(h * 128, 128)], load_sem.at[2 + i]).start()
        w_wait[i] = pltpu.make_async_copy(w1.at[i], w1.at[i], load_sem.at[2 + i])
    wd_load = pltpu.make_async_copy(down_hbm, wd, load_sem.at[1])
    wd_load.start()

    tok_load.wait()
    turned = jnp.swapaxes(tok[...], 0, 1)
    for ch in range(CHUNKS):
        side = []
        for c in range(NC):
            side.append(jnp.concatenate(
                [turned[(i * NC + c) * 64 + ch * 16:(i * NC + c) * 64 + ch * 16 + 16, :] for i in range(NX)], axis=0
            ))
        tok_all[ch, pl.ds(pl.multiple_of(gy * HALF, HALF), HALF)] = jnp.concatenate(side, axis=1)
    pl.semaphore_wait(barrier, len(peers))

    unsent = {}

    def flush(k):
        for copy in unsent.pop(k, ()):
            copy.wait_send()

    class Gather:
        def __init__(self, ref, ch, ways, cut, size, received, sems, k):
            self.ref, self.ch, self.size, self.received, self.sems, self.k = ref, ch, size, received, sems[ch], k
            self.groups, self.trees = ways
            self.parts = ((0, cut), (cut, size - cut))

        def rows_of(self, count, g):
            rows = self.ref.at[self.ch, pl.ds(0, count)]
            return remote(rows, rows, send_sem.at[self.k], self.received.at[self.sems + g], at(dy=1))

        def step(self, g):
            group = self.groups[g]
            if g == 0:
                unsent[self.k] = [self.rows_of((NY * NZ - 1) * self.size, 0)]
            else:
                self.rows_of(sum(self.parts[part][1] for part, _, _ in group), g - 1).wait_recv()
            moves = []
            for part, block, nexts in group:
                slot = slot_of(*block)
                first, count = self.parts[part]
                rows = self.ref.at[self.ch, pl.ds(pl.multiple_of(slot * self.size + first, 16), count)]
                for after in nexts:
                    dy, dz = wrap(block[0] - after[0], NY), wrap(block[1] - after[1], NZ)
                    moves.append((-depth_of(self.trees[part], after), rows, at(dy=dy, dz=dz), self.arrives(part, after)))
            moves.sort(key=lambda move: move[0])
            for _, rows, device, there in moves:
                remote(rows, rows, send_sem.at[self.k], self.received.at[self.sems + there - 1], device).start()

        def arrives(self, part, block):
            for g, group in enumerate(self.groups):
                if any(p == part and b == block for p, b, _ in group):
                    return g

    tok_gather = [Gather(tok_all, ch, TOK_WAYS[ch], TOK_CUTS[ch], HALF, tok_recv, TOK_SEMS, ch) for ch in range(CHUNKS)]
    hid_gather = [Gather(hid_all, ch, HID_WAYS[ch], HID_CUTS[ch], ROWS, hid_recv, HID_SEMS, CHUNKS + ch) for ch in range(CHUNKS)]

    def send_parts(ch, i):
        return remote(part_out.at[ch, i], part_in.at[ch, i], send_sem.at[2 * CHUNKS + ch], part_recv.at[ch, i], at(dc=1))

    def send_sum(ch, i):
        k = 3 * CHUNKS + ch
        return remote(sum_out.at[ch, i - 1], sum_in.at[ch, i - 1], send_sem.at[k], sum_recv.at[ch], at(dx=i))

    def tok_step(ch, s):
        tok_gather[ch].step(s)

    def pack(ch, _):
        for a in range(0, NY * NZ, 2):
            lo, hi = tok_all[ch, a * HALF:(a + 1) * HALF], tok_all[ch, (a + 1) * HALF:(a + 2) * HALF]
            columns = slice(a * 64, a * 64 + 128)
            lhs[LHS[ch], :HALF, columns] = jnp.concatenate([lo[:, :64], hi[:, :64]], axis=1)
            lhs[LHS[ch], HALF:, columns] = jnp.concatenate([lo[:, 64:], hi[:, 64:]], axis=1)

    def theirs(ch, i):
        if ch == 0:
            w_wait[i].wait()
        part_out[ch, i] = jnp.dot(lhs[LHS[ch]], w1[i], preferred_element_type=jnp.float32)
        send_parts(ch, i).start()
        if i == 0:
            unsent[2 * CHUNKS + ch] = [remote(part_out.at[ch], part_in.at[ch], send_sem.at[2 * CHUNKS + ch], part_recv.at[ch, i], at(dc=1))]

    def mine(ch, i):
        if ch == 0:
            w_wait[4 + i].wait()
        total = jnp.dot(lhs[LHS[ch]], w1[4 + i], preferred_element_type=jnp.float32)
        send_parts(ch, i).wait_recv()
        total = total + part_in[ch, i]
        if i == 0:
            own[ch] = total
        else:
            sum_out[ch, i - 1] = total.astype(jnp.bfloat16)
            send_sum(ch, i).start()

    def activate(ch, _):
        k = 3 * CHUNKS + ch
        sums = remote(sum_out.at[ch], sum_in.at[ch], send_sem.at[k], sum_recv.at[ch], at(dx=1))
        unsent[k] = [sums]
        sums.wait_recv()
        total = own[ch]
        for i in range(3):
            total = total + sum_in[ch, i].astype(jnp.float32)
        gate, up = total[:, :128], total[:, 128:]
        hid_all[ch, pl.ds(pl.multiple_of(gy * ROWS, ROWS), ROWS)] = (gate / (1.0 + jnp.exp(-gate)) * up).astype(jnp.bfloat16)
        hid_gather[ch].step(0)

    def hid_step(ch, s):
        hid_gather[ch].step(s)

    def mix(ch, _):
        if ch == 0:
            wd_load.wait()
        rows = jnp.concatenate([hid_all[ch, a * ROWS:(a + 1) * ROWS] for a in range(NY * NZ)], axis=1)
        total = jnp.dot(rows, wd[...].reshape(NY * NZ * 128, 512), preferred_element_type=jnp.float32)
        acc[ch] = total
        red_out[ch] = total.astype(jnp.bfloat16)
        for k, (dx, dc) in enumerate(((2, 0), (2, 1), (1, 0), (1, 1), (3, 0), (3, 1), (0, 1))):
            place = (core + dc) % NC * HALF + (x + dx) % NX * 16
            part = red_out.at[ch, pl.ds(pl.multiple_of(place, 16), 16)]
            there = red_in.at[ch, pl.ds(k * 16, 16)]
            remote(part, there, send_sem.at[4 * CHUNKS + ch], red_recv.at[ch], at(dx=dx, dc=dc)).start()
        unsent[4 * CHUNKS + ch] = [all_reduced(ch)]

    def all_reduced(ch):
        return remote(red_out.at[ch, pl.ds(0, 7 * 16)], red_in.at[ch], send_sem.at[4 * CHUNKS + ch], red_recv.at[ch], at(dc=1))

    def finish(ch, _):
        all_reduced(ch).wait_recv()
        total = acc[ch, pl.ds(pl.multiple_of(core * HALF + x * 16, 16), 16), :]
        for k in range(7):
            total = total + red_in[ch, k * 16:(k + 1) * 16].astype(jnp.float32)
        out_ref[ch * 16:(ch + 1) * 16, :] = total.astype(jnp.bfloat16)

    actions = {
        "tok": tok_step, "pack": pack, "theirs": theirs, "mine": mine, "act": activate, "hid": hid_step,
        "mix": mix, "finish": finish,
    }
    for name, ch, step in ORDER:
        actions[name](ch, step)

    for k in list(unsent):
        flush(k)


def body(tokens, gate_weight, up_weight, down_weight):
    bf16, f32 = jnp.bfloat16, jnp.float32
    return pl.pallas_call(
        kernel,
        out_shape=pltpu.VMEM((64, 512), bf16),
        in_specs=[pl.BlockSpec(memory_space=pl.ANY)] * 4,
        out_specs=pl.BlockSpec(memory_space=pltpu.VMEM),
        scratch_shapes=[
            pltpu.VMEM((64, 512), bf16),
            pltpu.VMEM((8, 2048, 256), bf16),
            pltpu.VMEM((32, 128, 512), bf16),
            pltpu.VMEM((CHUNKS, NY * NZ * HALF, 128), bf16),
            pltpu.VMEM((2, ROWS, 2048), bf16),
            pltpu.VMEM((CHUNKS, ROWS, 256), f32),
            pltpu.VMEM((CHUNKS, 4, ROWS, 256), f32),
            pltpu.VMEM((CHUNKS, 4, ROWS, 256), f32),
            pltpu.VMEM((CHUNKS, 3, ROWS, 256), bf16),
            pltpu.VMEM((CHUNKS, 3, ROWS, 256), bf16),
            pltpu.VMEM((CHUNKS, NY * NZ * ROWS, 128), bf16),
            pltpu.VMEM((CHUNKS, ROWS, 512), f32),
            pltpu.VMEM((CHUNKS, ROWS, 512), bf16),
            pltpu.VMEM((CHUNKS, 7 * 16, 512), bf16),
            pltpu.SemaphoreType.DMA((10,)),
            pltpu.SemaphoreType.DMA((TOK_SEMS[-1],)),
            pltpu.SemaphoreType.DMA((HID_SEMS[-1],)),
            pltpu.SemaphoreType.DMA((CHUNKS, 4)),
            pltpu.SemaphoreType.DMA((CHUNKS,)),
            pltpu.SemaphoreType.DMA((CHUNKS,)),
            pltpu.SemaphoreType.DMA((5 * CHUNKS,)),
        ],
        compiler_params=pltpu.CompilerParams(
            collective_id=0, has_side_effects=True, vmem_limit_bytes=56 * 1024 * 1024
        ),
        cost_estimate=pl.CostEstimate(flops=6442450944, bytes_accessed=12 << 20, transcendentals=0),
    )(tokens.T, gate_weight, up_weight, down_weight)


def solution(mesh):
    in_specs = (P(None, ("gx", "gy")), P("gx", "gy"), P("gx", "gy"), P(None, "gx", "gy"))
    return jax.shard_map(body, mesh=mesh, in_specs=in_specs, out_specs=P("gx", "gy"), check_vma=False)
```
